1024 devices in a mesh: pair: 64 (over x, z), virt: 16 (over y, core).
Axes of the slice: x: 8, y: 8, z: 8, core: 2. Of those that a mesh axis runs over, the one named last changes fastest.
Arguments:
- amplitudes: bfloat16 [4096, 128, 128], P('pair'), as said below
- factors: bfloat16 [64, 128, 128], P(None, 'virt'), may hold values from -0.1875 to 0.1875
- ov_factors: bfloat16 [64, 64, 128], replicated, may hold values from -0.15625 to 0.15625
- fock_matrix: bfloat16 [128, 128], replicated, may hold values from -0.5 to 0.5
- screen: int32 [64, 64], P('pair'), may hold values 0 or 1
Outputs:
- residual: bfloat16 [4096, 128, 128], P('pair', 'virt')
The draws below stay inside these ranges and needn't reach their ends.
Inputs may be any that keep to these rules, and one draw needn't show every extreme that they name: amplitudes[(j,i), c, d] = amplitudes[(i,j), d, c] for all pairs.
All inputs are finite; a program needn't handle non-finite values. No bound on the sum of `screen` on one device may be relied on, other than what follows from the above.
Results may differ from the reference program's by a relative error of at most 0.0095.
Values may be sent and summed in bfloat16 or wider, within the bound.
A program may use at most 32 MiB of HBM per device.

```python
import jax
import jax.numpy as jnp
from jax import lax

V = 128
Q = 64
NOCC = 64


def draw_amplitudes(key, part):
    key = jax.random.fold_in(key, 11)
    base = jax.random.normal(key, (NOCC, NOCC, V, V), jnp.float32)
    swapped = base.transpose(1, 0, 3, 2)
    inner = (base + base.transpose(0, 1, 3, 2)) * 0.7071
    first = jnp.arange(NOCC)[:, None, None, None]
    second = jnp.arange(NOCC)[None, :, None, None]
    joined = jnp.where(first < second, base, jnp.where(first > second, swapped, inner))
    return joined.reshape(NOCC * NOCC, V, V).astype(jnp.bfloat16)


def touch_ends(array, rng, low, largest):
    dims = array.shape
    spot = [jax.random.randint(jax.random.fold_in(rng, axis), (), 0, dims[axis]) for axis in range(len(dims))]
    array = array.at[tuple(spot)].set(low)
    longest = dims.index(max(dims))
    spot[longest] = (spot[longest] + 1) % dims[longest]
    return array.at[tuple(spot)].set(largest)


def shard_levels(key, dims, split, smallest, top_value):
    level, own = 1.0, jax.random.fold_in(key, 6)
    for dim, shards_of in split:
        draws = jnp.exp(jax.random.uniform(jax.random.fold_in(own, dim), (shards_of,), jnp.float32, smallest / len(split), top_value / len(split)))
        level = level * jnp.repeat(draws, dims[dim] // shards_of).reshape([-1 if axis == dim else 1 for axis in range(len(dims))])
    return level


def scatter_about(stream_key, dims, scale, most, split=(), held_as=jnp.bfloat16):
    factor_of = shard_levels(stream_key, dims, split, -0.22, 0.18) if split else 1.0
    values = jax.random.normal(stream_key, dims, jnp.float32) * scale * factor_of
    return jnp.minimum(jnp.maximum(values, -most), most).astype(held_as)


def setup_inputs(seed: int = 0) -> dict:
    seeds = jax.random.split(jax.random.key(seed), 6)
    return {
        "amplitudes": draw_amplitudes(jax.random.fold_in(seeds[5], 71), 0),
        "factors": scatter_about(seeds[1], (Q, V, V), (8 * V) ** -0.5, 0.1875, ((1, 16),)),
        "ov_factors": scatter_about(seeds[2], (Q, NOCC, V), (2 * (NOCC * V * Q) ** 0.5) ** -0.5, 0.15625),
        "fock_matrix": scatter_about(seeds[3], (V, V), V ** -0.5, 0.5),
        "screen": touch_ends((jax.random.randint(seeds[4], (NOCC, NOCC), 0, 4) < 3).astype(jnp.int32), jax.random.fold_in(seeds[4], 1), 0, 1),
    }


def reference(amplitudes, factors, ov_factors, fock_matrix, screen):
    occ_count = screen.shape[0]
    virt_width = fock_matrix.shape[0]
    amp_grid = amplitudes.reshape(occ_count, occ_count, virt_width, virt_width)
    factor_wide = factors.astype(jnp.float32)

    def ladder_block(block):
        intermediate = jnp.einsum('pcd,qbd->pqbc', block.astype(jnp.float32), factor_wide).astype(jnp.bfloat16)
        return jnp.einsum('qac,pqbc->pab', factor_wide, intermediate.astype(jnp.float32)).astype(jnp.bfloat16)

    ladder = lax.map(ladder_block, amp_grid)
    amp_wide = amp_grid.astype(jnp.float32)
    ov_wide = ov_factors.astype(jnp.float32)
    dressed = 2.0 * jnp.einsum('ikac,pkc->iap', amp_wide, ov_wide) - jnp.einsum('ikca,pkc->iap', amp_wide, ov_wide)
    dressed = dressed.astype(jnp.bfloat16).astype(jnp.float32)
    cycle = jnp.einsum('iap,pjb->ijab', dressed, ov_wide).astype(jnp.bfloat16)
    mirror = cycle.transpose(1, 0, 3, 2)
    fock_wide = fock_matrix.astype(jnp.float32)
    fock_term = jnp.einsum('ijac,cb->ijab', amp_wide, fock_wide) + jnp.einsum('ac,ijcb->ijab', fock_wide, amp_wide)
    weight = screen.astype(jnp.float32)[:, :, None, None]
    total = weight * (ladder.astype(jnp.float32) + cycle.astype(jnp.float32) + mirror.astype(jnp.float32) + fock_term)
    return total.transpose(0, 1, 3, 2).reshape(occ_count * occ_count, virt_width, virt_width).astype(jnp.bfloat16)
```

```python
import jax
import jax.numpy as jnp
from jax import lax
from jax.experimental import pallas as pl
from jax.experimental.pallas import tpu as pltpu
from jax.sharding import PartitionSpec as P

F32, BF16 = jnp.float32, jnp.bfloat16
MESH = pl.DeviceIdType.MESH
NX, NY, NZ = 8, 8, 8
V, Q, NOCC, W = 128, 64, 64, 8
QROWS = Q // 4 * W
HALF = QROWS // 2
ORDER = (1, 7, 2, 6, 3, 5, 4)


def dot_nt(a, b):
    return lax.dot_general(a, b, (((1,), (1,)), ((), ())), preferred_element_type=F32)


def dot_nn(a, b):
    return jnp.dot(a, b, preferred_element_type=F32)


def kernel(
    amp_hbm, fac_hbm, ov_hbm, fock_hbm, screen_hbm, out_ref,
    amp, ov_raw, ov_wide, ov_by_k, fock, screen, lhs, gathered, inter, weights,
    g_near, g_pack, g_far,
    local_sem, y_send, y_recv, in_send, in_recv, sib_send, sib_recv, own_sem, g_sem,
):
    pair, virt = lax.axis_index("pair"), lax.axis_index("virt")
    x, z = pair // NZ, pair % NZ
    y, core = virt // 2, virt % 2
    color = (x + 2 * z) % 4
    sibling = (pair, y * 2 + 1 - core)

    def rows(quarter):
        return pl.ds(pl.multiple_of(quarter % 4 * QROWS, QROWS), QROWS)

    def half_rows(quarter, half):
        return pl.ds(pl.multiple_of(quarter % 4 * QROWS + half * HALF, HALF), HALF)

    def remote(src, dst, send, recv, device):
        return pltpu.make_async_remote_copy(
            src_ref=src, dst_ref=dst, send_sem=send, recv_sem=recv, device_id=device, device_id_type=MESH
        )

    loads = [
        pltpu.make_async_copy(ov_hbm, ov_raw, local_sem.at[0]),
        pltpu.make_async_copy(amp_hbm, amp, local_sem.at[1]),
        pltpu.make_async_copy(fock_hbm, fock, local_sem.at[2]),
        pltpu.make_async_copy(fac_hbm, lhs.at[pl.ds(0, Q * W)], local_sem.at[3]),
        pltpu.make_async_copy(fac_hbm, gathered.at[virt], local_sem.at[4]),
        pltpu.make_async_copy(screen_hbm, screen, local_sem.at[5]),
    ]
    for load in loads:
        load.start()

    barrier = pltpu.get_barrier_semaphore()
    peers = [(pair, (y + d) % NY * 2 + core) for d in ORDER]
    peers += [sibling]
    peers += [((x + d) % NX * NZ + z, virt) for d in range(1, NX)]
    peers += [(x * NZ + (z + d) % NZ, virt) for d in range(1, NZ)]
    for peer in peers:
        pl.semaphore_signal(barrier, inc=1, device_id=peer, device_id_type=MESH)

    loads[0].wait()
    ov_wide[...] = ov_raw[...].astype(F32)

    def split_k(k, carry):
        ov_by_k[k] = ov_wide[pl.ds(k, Q, stride=NOCC), :].astype(BF16)
        return carry

    lax.fori_loop(0, NOCC, split_k, 0, unroll=8)
    loads[1].wait()

    def dress(k, carry):
        direct, crossed = carry
        left = jnp.concatenate([ov_by_k[2 * k], ov_by_k[2 * k + 1]], axis=1)
        pair_rows = amp[pl.ds(pl.multiple_of(k * 2 * V, 2 * V), 2 * V), :]
        side = jnp.concatenate([pair_rows[:V], pair_rows[V:]], axis=1)
        return direct + dot_nt(left, side), crossed + dot_nn(left, pair_rows)

    zero = jnp.zeros((Q, V), F32)
    direct, crossed = lax.fori_loop(0, NOCC // 2, dress, (zero, zero), unroll=4)
    dressed = (2.0 * direct - crossed).astype(BF16)
    lane = lax.broadcasted_iota(jnp.int32, (16, V), 1)
    line = lax.broadcasted_iota(jnp.int32, (16, V), 0)
    chip_rows = jnp.where(lane == y * 16 + line, 1.0, 0.0).astype(BF16)
    mine = dot_nt(chip_rows, dressed)
    mine = jnp.concatenate([mine, jnp.zeros((16, V - Q), F32)], axis=1).astype(BF16)
    g_near[x] = mine

    pl.semaphore_wait(barrier, len(peers))

    sends = []

    def start(copy):
        copy.start()
        sends.append(copy)

    for d in ORDER:
        start(
            remote(
                fac_hbm.at[rows(color)], gathered.at[virt, rows(color)],
                y_send.at[d - 1], y_recv.at[d - 1], (pair, (y + d) % NY * 2 + core),
            )
        )
    start(remote(fac_hbm, gathered.at[virt], own_sem.at[0], own_sem.at[1], sibling))
    for d in range(1, NX):
        start(
            remote(
                g_near.at[x], g_near.at[x], g_sem.at[0, d - 1], g_sem.at[1, d - 1],
                ((x + d) % NX * NZ + z, virt),
            )
        )

    loads[2].wait()
    loads[3].wait()
    own_rows = jnp.where(lane == virt * W + line % W, 1.0, 0.0)
    fock_rows = dot_nt(own_rows.astype(BF16), fock[...])
    lhs[pl.ds(Q * W, 16), :] = jnp.where(line < W, fock_rows, own_rows).astype(BF16)

    def inter_step(jp, carry):
        both = dot_nt(lhs[...], amp[pl.ds(pl.multiple_of(jp * 2 * V, 2 * V), 2 * V), :])
        both = both.reshape(Q + 2, W, 2 * V)
        packed = jnp.concatenate([both[:, :, :V], both[:, :, V:]], axis=1).astype(BF16)
        inter[:, pl.ds(pl.multiple_of(jp * 16, 16), 16), :] = packed
        return carry

    def from_y(d):
        return (y - d) % NY * 2 + core

    def relay(d):
        slot, quarter = from_y(d), rows(color)
        piece = gathered.at[slot, quarter]
        remote(piece, piece, y_send.at[d - 1], y_recv.at[d - 1], sibling).wait_recv()
        start(remote(piece, piece, in_send.at[d - 1, 4], in_recv.at[d - 1, 4], sibling))
        for way, (dx, dz) in enumerate(((1, 0), (-1, 0), (0, 1), (0, -1))):
            part = piece if way < 2 else gathered.at[slot, half_rows(color, way - 2)]
            target = ((x + dx) % NX * NZ + (z + dz) % NZ, virt)
            start(remote(part, part, in_send.at[d - 1, way], in_recv.at[d - 1, way], target))

    def relay_in_plane(d):
        slot = from_y(d)
        for way, quarter in enumerate((rows(color + 3), rows(color + 1), half_rows(color + 2, 0), half_rows(color + 2, 1))):
            part = gathered.at[slot, quarter]
            remote(part, part, in_send.at[d - 1, way], in_recv.at[d - 1, way], sibling).wait_recv()
        for n in range(3):
            part = gathered.at[slot, rows(color + 1 + n)]
            start(remote(part, part, sib_send.at[d - 1, n], sib_recv.at[d - 1, n], sibling))

    steps = NOCC // 2
    for n, group in enumerate(((1, 7), (2, 6), (3, 5), (4,))):
        lax.fori_loop(steps // 4 * n, steps // 4 * (n + 1), inter_step, 0, unroll=8)
        for d in group:
            relay(d)

    for d in range(1, NX):
        there = g_near.at[(x - d) % NX]
        remote(there, there, g_sem.at[0, d - 1], g_sem.at[1, d - 1], sibling).wait_recv()

    def near_rows(n):
        wide = g_near[n].astype(F32)
        return jnp.where(core == 0, wide[:W], wide[W:])

    for m in range(NX // 2):
        low, high = near_rows(m), near_rows(m + NX // 2)
        both = jnp.concatenate([low[:, :Q], high[:, :Q]], axis=1)
        g_pack[pl.ds(m * W, W), :] = both
    g_far[z] = g_pack[...].astype(BF16)
    for d in range(1, NZ):
        start(
            remote(
                g_far.at[z], g_far.at[z], g_sem.at[2, d - 1], g_sem.at[3, d - 1],
                (x * NZ + (z + d) % NZ, virt),
            )
        )
    for d in ORDER:
        relay_in_plane(d)

    picked = []
    own_mat = own_rows.astype(BF16)
    for n in range(NOCC // 4):
        four = dot_nt(own_mat, ov_by_k[4 * n : 4 * n + 4].reshape(4 * Q, V))[:W]
        picked += [four[:, :V], four[:, V:]]
    picked = jnp.concatenate(picked, axis=0).astype(BF16)

    def twice(block):
        empty = jnp.zeros((Q, V), BF16)
        top = jnp.concatenate([block, empty], axis=1)
        return jnp.concatenate([top, jnp.concatenate([empty, block], axis=1)], axis=0)

    cycle = dot_nn(picked, twice(dressed)).reshape(NOCC // 2, W, 2 * V)
    ov_mine = ov_wide[pl.ds(pair, Q, stride=NOCC), :].astype(BF16)

    def regroup(chip):
        first = gathered[chip * 2].astype(F32).reshape(Q, W, V)
        second = gathered[chip * 2 + 1].astype(F32).reshape(Q, W, V)
        weights[:, pl.ds(pl.multiple_of(chip * 16, 16), 16), :] = jnp.concatenate([first, second], axis=1).astype(BF16)

    loads[4].wait()
    other = gathered.at[y * 2 + 1 - core]
    remote(other, other, own_sem.at[0], own_sem.at[1], sibling).wait_recv()
    regroup(y)
    for d in ORDER:
        slot = (y - d) % NY * 2 + 1 - core
        part = gathered.at[slot, rows(color)]
        remote(part, part, in_send.at[d - 1, 4], in_recv.at[d - 1, 4], sibling).wait_recv()
        for n in range(3):
            part = gathered.at[slot, rows(color + 1 + n)]
            remote(part, part, sib_send.at[d - 1, n], sib_recv.at[d - 1, n], sibling).wait_recv()
        regroup((y - d) % NY)

    total = dot_nt(inter[Q + 1], fock[...]) + inter[Q].astype(F32)
    for p in range(0, Q, 2):
        left = jnp.concatenate([inter[p], inter[p + 1]], axis=1)
        right = jnp.concatenate([weights[p], weights[p + 1]], axis=1)
        total = total + dot_nt(left, right)
    total = total.reshape(NOCC, W, V)

    for d in range(1, NZ):
        there = g_far.at[(z - d) % NZ]
        remote(there, there, g_sem.at[2, d - 1], g_sem.at[3, d - 1], sibling).wait_recv()
    mirror = dot_nn(g_far[...].reshape(NZ * NX // 2 * W, V), twice(ov_mine))
    mirror = mirror.reshape(NZ, NX // 2, W, 2 * V)

    loads[5].wait()
    for j in range(0, NOCC, 2):
        tiles = []
        for k in (j, j + 1):
            jx, jz = k // NZ, k % NZ
            lanes = slice(jx // (NX // 2) * V, (jx // (NX // 2) + 1) * V)
            tile = total[k] + cycle[k // 2, :, k % 2 * V : (k % 2 + 1) * V]
            tile = tile + mirror[jz, jx % (NX // 2), :, lanes]
            tiles.append(tile * screen[0, k].astype(F32))
        out_ref[pl.ds(j * W, 16), :] = jnp.concatenate(tiles, axis=0).astype(BF16)

    for copy in sends:
        copy.wait_send()


def body(amplitudes, factors, ov_factors, fock_matrix, screen):
    vmem, dma = pltpu.VMEM, pltpu.SemaphoreType.DMA
    out = pl.pallas_call(
        kernel,
        out_shape=jax.ShapeDtypeStruct((NOCC * W, V), BF16),
        in_specs=[pl.BlockSpec(memory_space=pl.ANY)] * 5,
        out_specs=pl.BlockSpec(memory_space=pltpu.VMEM),
        scratch_shapes=[
            vmem((NOCC * V, V), BF16),
            vmem((Q * NOCC, V), BF16),
            vmem((Q * NOCC, V), F32),
            vmem((NOCC, Q, V), BF16),
            vmem((V, V), BF16),
            pltpu.SMEM((1, NOCC), jnp.int32),
            vmem(((Q + 2) * W, V), BF16),
            vmem((NY * 2, Q * W, V), BF16),
            vmem((Q + 2, NOCC * W, V), BF16),
            vmem((Q, V, V), BF16),
            vmem((NX, 16, V), BF16),
            vmem((NX // 2 * W, V), F32),
            vmem((NZ, NX // 2 * W, V), BF16),
            dma((6,)),
            dma((NY - 1,)),
            dma((NY - 1,)),
            dma((NY - 1, 5)),
            dma((NY - 1, 5)),
            dma((NY - 1, 3)),
            dma((NY - 1, 3)),
            dma((2,)),
            dma((4, NX - 1)),
        ],
        compiler_params=pltpu.CompilerParams(
            collective_id=0, has_side_effects=True, vmem_limit_bytes=48 * 1024 * 1024
        ),
        name="residual",
    )(
        amplitudes.reshape(NOCC * V, V),
        factors.reshape(Q * W, V),
        ov_factors.reshape(Q * NOCC, V),
        fock_matrix,
        screen,
    )
    return out.reshape(NOCC, W, V)


def solution(mesh):
    in_specs = (P("pair", None, None), P(None, "virt", None), P(), P(), P("pair", None))
    out_specs = P("pair", "virt", None)
    return jax.shard_map(body, mesh=mesh, in_specs=in_specs, out_specs=out_specs, check_vma=False)
```

```python
import jax
import jax.numpy as jnp
from jax import lax
from jax.experimental import pallas as pl
from jax.experimental.pallas import tpu as pltpu
from jax.sharding import PartitionSpec as P

F32, BF16 = jnp.float32, jnp.bfloat16
MESH = pl.DeviceIdType.MESH
NX, NY, NZ = 8, 8, 8
V, Q, NOCC, W = 128, 64, 64, 8
QROWS = Q // 4 * W
HALF = QROWS // 2
ORDER = (1, 7, 2, 6, 3, 5, 4)


def dot_nt(a, b):
    return lax.dot_general(a, b, (((1,), (1,)), ((), ())), preferred_element_type=F32)


def dot_nn(a, b):
    return jnp.dot(a, b, preferred_element_type=F32)


def kernel(
    amp_hbm, fac_hbm, ov_hbm, fock_hbm, screen_hbm, out_ref,
    amp, ov_raw, ov_wide, ov_by_k, fock, screen, lhs, gathered, inter, weights,
    total, g_near, g_pack, g_far,
    local_sem, y_send, y_recv, in_send, in_recv, sib_send, sib_recv, own_sem, g_sem,
):
    pair, virt = lax.axis_index("pair"), lax.axis_index("virt")
    x, z = pair // NZ, pair % NZ
    y, core = virt // 2, virt % 2
    color = (x + 2 * z) % 4
    sibling = (pair, y * 2 + 1 - core)

    def rows(quarter):
        return pl.ds(pl.multiple_of(quarter % 4 * QROWS, QROWS), QROWS)

    def half_rows(quarter, half):
        return pl.ds(pl.multiple_of(quarter % 4 * QROWS + half * HALF, HALF), HALF)

    def remote(src, dst, send, recv, device):
        return pltpu.make_async_remote_copy(
            src_ref=src, dst_ref=dst, send_sem=send, recv_sem=recv, device_id=device, device_id_type=MESH
        )

    loads = [
        pltpu.make_async_copy(ov_hbm, ov_raw, local_sem.at[0]),
        pltpu.make_async_copy(amp_hbm, amp, local_sem.at[1]),
        pltpu.make_async_copy(fock_hbm, fock, local_sem.at[2]),
        pltpu.make_async_copy(fac_hbm, lhs.at[pl.ds(0, Q * W)], local_sem.at[3]),
        pltpu.make_async_copy(fac_hbm, gathered.at[virt], local_sem.at[4]),
        pltpu.make_async_copy(screen_hbm, screen, local_sem.at[5]),
    ]
    for load in loads:
        load.start()

    barrier = pltpu.get_barrier_semaphore()
    peers = [(pair, (y + d) % NY * 2 + core) for d in ORDER]
    peers += [sibling]
    peers += [((x + d) % NX * NZ + z, virt) for d in range(1, NX)]
    peers += [(x * NZ + (z + d) % NZ, virt) for d in range(1, NZ)]
    for peer in peers:
        pl.semaphore_signal(barrier, inc=1, device_id=peer, device_id_type=MESH)

    pl.semaphore_wait(barrier, len(peers))

    sends = []

    def start(copy):
        copy.start()
        sends.append(copy)

    for d in ORDER:
        start(
            remote(
                fac_hbm.at[rows(color)], gathered.at[virt, rows(color)],
                y_send.at[d - 1], y_recv.at[d - 1], (pair, (y + d) % NY * 2 + core),
            )
        )
    start(remote(fac_hbm, gathered.at[virt], own_sem.at[0], own_sem.at[1], sibling))
    def from_y(d):
        return (y - d) % NY * 2 + core

    def relay(d):
        slot, quarter = from_y(d), rows(color)
        piece = gathered.at[slot, quarter]
        remote(piece, piece, y_send.at[d - 1], y_recv.at[d - 1], sibling).wait_recv()
        start(remote(piece, piece, in_send.at[d - 1, 4], in_recv.at[d - 1, 4], sibling))
        for way, (dx, dz) in enumerate(((1, 0), (-1, 0), (0, 1), (0, -1))):
            part = piece if way < 2 else gathered.at[slot, half_rows(color, way - 2)]
            target = ((x + dx) % NX * NZ + (z + dz) % NZ, virt)
            start(remote(part, part, in_send.at[d - 1, way], in_recv.at[d - 1, way], target))

    def relay_in_plane(d):
        slot = from_y(d)
        for way, quarter in enumerate((rows(color + 3), rows(color + 1), half_rows(color + 2, 0), half_rows(color + 2, 1))):
            part = gathered.at[slot, quarter]
            remote(part, part, in_send.at[d - 1, way], in_recv.at[d - 1, way], sibling).wait_recv()
        for n in range(3):
            part = gathered.at[slot, rows(color + 1 + n)]
            start(remote(part, part, sib_send.at[d - 1, n], sib_recv.at[d - 1, n], sibling))

    loads[0].wait()
    ov_wide[...] = ov_raw[...].astype(F32)

    def split_k(k, carry):
        ov_by_k[k] = ov_wide[pl.ds(k, Q, stride=NOCC), :].astype(BF16)
        return carry

    lax.fori_loop(0, NOCC, split_k, 0, unroll=8)
    relay(1)
    relay(7)
    loads[1].wait()

    def dress(k, carry):
        direct, crossed = carry
        left = jnp.concatenate([ov_by_k[2 * k], ov_by_k[2 * k + 1]], axis=1)
        pair_rows = amp[pl.ds(pl.multiple_of(k * 2 * V, 2 * V), 2 * V), :]
        side = jnp.concatenate([pair_rows[:V], pair_rows[V:]], axis=1)
        return direct + dot_nt(left, side), crossed + dot_nn(left, pair_rows)

    zero = jnp.zeros((Q, V), F32)
    direct, crossed = lax.fori_loop(0, NOCC // 2, dress, (zero, zero), unroll=4)
    dressed = (2.0 * direct - crossed).astype(BF16)
    lane = lax.broadcasted_iota(jnp.int32, (16, V), 1)
    line = lax.broadcasted_iota(jnp.int32, (16, V), 0)
    chip_rows = jnp.where(lane == y * 16 + line, 1.0, 0.0).astype(BF16)
    mine = dot_nt(chip_rows, dressed)
    mine = jnp.concatenate([mine, jnp.zeros((16, V - Q), F32)], axis=1).astype(BF16)
    g_near[x] = mine

    for d in range(1, NX):
        start(
            remote(
                g_near.at[x], g_near.at[x], g_sem.at[0, d - 1], g_sem.at[1, d - 1],
                ((x + d) % NX * NZ + z, virt),
            )
        )

    loads[2].wait()
    loads[3].wait()
    own_rows = jnp.where(lane == virt * W + line % W, 1.0, 0.0)
    fock_rows = dot_nt(own_rows.astype(BF16), fock[...])
    lhs[pl.ds(Q * W, 16), :] = jnp.where(line < W, fock_rows, own_rows).astype(BF16)

    def inter_step(jp, carry):
        both = dot_nt(lhs[...], amp[pl.ds(pl.multiple_of(jp * 2 * V, 2 * V), 2 * V), :])
        both = both.reshape(Q + 2, W, 2 * V)
        packed = jnp.concatenate([both[:, :, :V], both[:, :, V:]], axis=1).astype(BF16)
        inter[:, pl.ds(pl.multiple_of(jp * 16, 16), 16), :] = packed
        return carry

    part = NOCC // 8
    lax.fori_loop(0, part, inter_step, 0, unroll=8)
    relay(2)
    relay(6)
    lax.fori_loop(part, 2 * part, inter_step, 0, unroll=8)
    relay(3)
    relay(5)
    relay_in_plane(1)
    relay_in_plane(7)
    lax.fori_loop(2 * part, 3 * part, inter_step, 0, unroll=8)
    relay(4)
    relay_in_plane(2)
    relay_in_plane(6)
    lax.fori_loop(3 * part, 4 * part, inter_step, 0, unroll=8)
    relay_in_plane(3)
    relay_in_plane(5)

    picked = []
    own_mat = own_rows.astype(BF16)
    for n in range(NOCC // 4):
        four = dot_nt(own_mat, ov_by_k[4 * n : 4 * n + 4].reshape(4 * Q, V))[:W]
        picked += [four[:, :V], four[:, V:]]
    picked = jnp.concatenate(picked, axis=0).astype(BF16)

    def twice(block):
        empty = jnp.zeros((Q, V), BF16)
        top = jnp.concatenate([block, empty], axis=1)
        return jnp.concatenate([top, jnp.concatenate([empty, block], axis=1)], axis=0)

    cycle = dot_nn(picked, twice(dressed)).reshape(NOCC // 2, W, 2 * V)
    ov_mine = ov_wide[pl.ds(pair, Q, stride=NOCC), :].astype(BF16)

    relay_in_plane(4)

    def ladder(quarter):
        span = rows(quarter)
        first = pl.multiple_of(quarter % 4 * (Q // 4), Q // 4)
        for chip in range(NY):
            one = gathered[2 * chip, span, :].astype(F32).reshape(Q // 4, W, V)
            two = gathered[2 * chip + 1, span, :].astype(F32).reshape(Q // 4, W, V)
            weights[pl.ds(first, Q // 4), chip * 16 : chip * 16 + 16, :] = jnp.concatenate([one, two], axis=1).astype(BF16)
        for m in range(0, NOCC * W, 256):
            block = None
            for p in range(0, Q // 4, 2):
                left = [inter[first + p + n, m : m + 256] for n in range(2)]
                right = [weights[first + p + n] for n in range(2)]
                term = dot_nt(jnp.concatenate(left, axis=1), jnp.concatenate(right, axis=1))
                block = term if block is None else block + term
            total[m : m + 256] += block

    for m in range(0, NOCC * W, 256):
        block = dot_nt(inter[Q + 1, m : m + 256], fock[...])
        total[m : m + 256] = block + inter[Q, m : m + 256].astype(F32)
    loads[4].wait()
    other = gathered.at[y * 2 + 1 - core]
    remote(other, other, own_sem.at[0], own_sem.at[1], sibling).wait_recv()
    for d in ORDER:
        there = gathered.at[(y - d) % NY * 2 + 1 - core, rows(color)]
        remote(there, there, in_send.at[d - 1, 4], in_recv.at[d - 1, 4], sibling).wait_recv()
    ladder(color)

    for d in range(1, NX):
        there = g_near.at[(x - d) % NX]
        remote(there, there, g_sem.at[0, d - 1], g_sem.at[1, d - 1], sibling).wait_recv()

    def near_rows(n):
        wide = g_near[n].astype(F32)
        return jnp.where(core == 0, wide[:W], wide[W:])

    for m in range(NX // 2):
        low, high = near_rows(m), near_rows(m + NX // 2)
        both = jnp.concatenate([low[:, :Q], high[:, :Q]], axis=1)
        g_pack[pl.ds(m * W, W), :] = both
    g_far[z] = g_pack[...].astype(BF16)
    for d in range(1, NZ):
        start(
            remote(
                g_far.at[z], g_far.at[z], g_sem.at[2, d - 1], g_sem.at[3, d - 1],
                (x * NZ + (z + d) % NZ, virt),
            )
        )
    for n in (1, 0, 2):
        for d in ORDER:
            there = gathered.at[(y - d) % NY * 2 + 1 - core, rows(color + 1 + n)]
            remote(there, there, sib_send.at[d - 1, n], sib_recv.at[d - 1, n], sibling).wait_recv()
        ladder(color + 1 + n)

    for d in range(1, NZ):
        there = g_far.at[(z - d) % NZ]
        remote(there, there, g_sem.at[2, d - 1], g_sem.at[3, d - 1], sibling).wait_recv()
    mirror = dot_nn(g_far[...].reshape(NZ * NX // 2 * W, V), twice(ov_mine))
    mirror = mirror.reshape(NZ, NX // 2, W, 2 * V)

    loads[5].wait()
    for j in range(0, NOCC, 2):
        tiles = []
        for k in (j, j + 1):
            jx, jz = k // NZ, k % NZ
            lanes = slice(jx // (NX // 2) * V, (jx // (NX // 2) + 1) * V)
            tile = total[k * W : (k + 1) * W] + cycle[k // 2, :, k % 2 * V : (k % 2 + 1) * V]
            tile = tile + mirror[jz, jx % (NX // 2), :, lanes]
            tiles.append(tile * screen[0, k].astype(F32))
        out_ref[pl.ds(j * W, 16), :] = jnp.concatenate(tiles, axis=0).astype(BF16)

    for copy in sends:
        copy.wait_send()


def body(amplitudes, factors, ov_factors, fock_matrix, screen):
    vmem, dma = pltpu.VMEM, pltpu.SemaphoreType.DMA
    out = pl.pallas_call(
        kernel,
        out_shape=jax.ShapeDtypeStruct((NOCC * W, V), BF16),
        in_specs=[pl.BlockSpec(memory_space=pl.ANY)] * 5,
        out_specs=pl.BlockSpec(memory_space=pltpu.VMEM),
        scratch_shapes=[
            vmem((NOCC * V, V), BF16),
            vmem((Q * NOCC, V), BF16),
            vmem((Q * NOCC, V), F32),
            vmem((NOCC, Q, V), BF16),
            vmem((V, V), BF16),
            pltpu.SMEM((1, NOCC), jnp.int32),
            vmem(((Q + 2) * W, V), BF16),
            vmem((NY * 2, Q * W, V), BF16),
            vmem((Q + 2, NOCC * W, V), BF16),
            vmem((Q, V, V), BF16),
            vmem((NOCC * W, V), F32),
            vmem((NX, 16, V), BF16),
            vmem((NX // 2 * W, V), F32),
            vmem((NZ, NX // 2 * W, V), BF16),
            dma((6,)),
            dma((NY - 1,)),
            dma((NY - 1,)),
            dma((NY - 1, 5)),
            dma((NY - 1, 5)),
            dma((NY - 1, 3)),
            dma((NY - 1, 3)),
            dma((2,)),
            dma((4, NX - 1)),
        ],
        compiler_params=pltpu.CompilerParams(
            collective_id=0, has_side_effects=True, vmem_limit_bytes=62 * 1024 * 1024
        ),
        name="residual",
    )(
        amplitudes.reshape(NOCC * V, V),
        factors.reshape(Q * W, V),
        ov_factors.reshape(Q * NOCC, V),
        fock_matrix,
        screen,
    )
    return out.reshape(NOCC, W, V)


def solution(mesh):
    in_specs = (P("pair", None, None), P(None, "virt", None), P(), P(), P("pair", None))
    out_specs = P("pair", "virt", None)
    return jax.shard_map(body, mesh=mesh, in_specs=in_specs, out_specs=out_specs, check_vma=False)
```

```python
import functools

import jax
import jax.numpy as jnp
from jax import lax
from jax.experimental import pallas as pl
from jax.experimental.pallas import tpu as pltpu
from jax.sharding import PartitionSpec as P

F32, BF16 = jnp.float32, jnp.bfloat16
MESH = pl.DeviceIdType.MESH
NX, NY, NZ = 8, 8, 8
V, Q, NOCC, W = 128, 64, 64, 8
QROWS = Q // 4 * W
PARTS = 4
ORDER = (1, 7, 2, 6, 3, 5, 4)


def dot_nt(a, b):
    return lax.dot_general(a, b, (((1,), (1,)), ((), ())), preferred_element_type=F32)


def dot_nn(a, b):
    return jnp.dot(a, b, preferred_element_type=F32)


def kernel(
    amp_hbm, fac_hbm, ov_hbm, fock_hbm, screen_hbm, out_ref,
    amp, ov_raw, ov_wide, ov_by_k, fock, screen, lhs, gathered, inter, weights,
    total, g_near, g_pack, g_far,
    local_sem, amp_sem, y_send, y_recv, in_send, in_recv, sib_send, sib_recv, own_sem, g_sem, ready,
):
    pair, virt = lax.axis_index("pair"), lax.axis_index("virt")
    x, z = pair // NZ, pair % NZ
    y, core = virt // 2, virt % 2
    color = (x + 2 * z) % 4
    sibling = (pair, y * 2 + 1 - core)

    def rows(quarter):
        return pl.ds(pl.multiple_of(quarter % 4 * QROWS, QROWS), QROWS)

    def remote(src, dst, send, recv, device):
        return pltpu.make_async_remote_copy(
            src_ref=src, dst_ref=dst, send_sem=send, recv_sem=recv, device_id=device, device_id_type=MESH
        )

    def amp_load(n):
        span = pl.ds(n * NOCC * V // PARTS, NOCC * V // PARTS)
        return pltpu.make_async_copy(amp_hbm.at[span], amp.at[span], amp_sem.at[n])

    ov_load = pltpu.make_async_copy(ov_hbm, ov_raw, local_sem.at[0])
    ov_load.start()
    for n in range(PARTS):
        amp_load(n).start()
    loads = [
        pltpu.make_async_copy(fock_hbm, fock, local_sem.at[2]),
        pltpu.make_async_copy(fac_hbm, lhs.at[pl.ds(0, Q * W)], local_sem.at[3]),
        pltpu.make_async_copy(fac_hbm, gathered.at[virt], local_sem.at[4]),
        pltpu.make_async_copy(screen_hbm, screen, local_sem.at[5]),
    ]
    for load in loads:
        load.start()

    def key(px, py, pz, pc):
        hops = jnp.minimum(px, NX - px) + jnp.minimum(py, NY - py)
        number = ((px * NZ + pz) * NY + py) * 2 + pc
        return jnp.where(number == 0, 9 * NZ // 2 * 1024 - 1, (pz * 9 + hops) * 1024 + number)

    mine = key(x, y, z, core)
    peers, answers, later = [], [], []
    for axis in range(3):
        for d in range(1, 8):
            at = [x, y, z]
            at[axis] = (at[axis] + d) % 8
            peers.append((at[0] * NZ + at[2], at[1] * 2 + core))
            answers.append(axis * 7 + 7 - d)
            later.append(key(*at, core) > mine)
    peers.append(sibling)
    answers.append(21)
    later.append(key(x, y, z, 1 - core) > mine)

    def signal(semaphore, device):
        pl.semaphore_signal(semaphore, inc=1, device_id=device, device_id_type=MESH)

    barrier = pltpu.get_barrier_semaphore()
    for peer, is_later in zip(peers, later):
        pl.when(is_later)(functools.partial(signal, barrier, peer))
    earlier_count = sum(jnp.where(is_later, 0, 1) for is_later in later)

    def ensure(slot):
        pl.when(later[slot])(functools.partial(pl.semaphore_wait, ready.at[slot], 1))

    def slot_of(axis, d):
        return axis * 7 + d - 1

    sends = []

    def start(copy):
        copy.start()
        sends.append((None, copy))

    def start_if(condition, copy):
        pl.when(condition)(copy.start)
        sends.append((condition, copy))

    def from_y(d):
        return (y - d) % NY * 2 + core

    def relay(d):
        slot, quarter = from_y(d), rows(color)
        piece = gathered.at[slot, quarter]
        remote(piece, piece, y_send.at[d - 1], y_recv.at[d - 1], sibling).wait_recv()
        start(remote(piece, piece, in_send.at[d - 1, 3], in_recv.at[d - 1, 3], sibling))
        for way, target in enumerate(((x + 1) % NX * NZ + z, (x + NX - 1) % NX * NZ + z, x * NZ + z + 1 - z % 2 * 2)):
            start(remote(piece, piece, in_send.at[d - 1, way], in_recv.at[d - 1, way], (target, virt)))

    def relay_in_plane(d):
        slot = from_y(d)
        for way, quarter in enumerate((rows(color + 3), rows(color + 1), rows(color + 2))):
            part = gathered.at[slot, quarter]
            remote(part, part, in_send.at[d - 1, way], in_recv.at[d - 1, way], sibling).wait_recv()
        for n in range(3):
            part = gathered.at[slot, rows(color + 1 + n)]
            start(remote(part, part, sib_send.at[d - 1, n], sib_recv.at[d - 1, n], sibling))

    ov_load.wait()
    ov_wide[...] = ov_raw[...].astype(F32)

    def split_k(k, carry):
        ov_by_k[k] = ov_wide[pl.ds(k, Q, stride=NOCC), :].astype(BF16)
        return carry

    lax.fori_loop(0, NOCC, split_k, 0, unroll=8)

    pl.when(earlier_count > 0)(functools.partial(pl.semaphore_wait, barrier, earlier_count))
    for slot in range(22):
        pl.when(jnp.logical_not(later[slot]))(functools.partial(signal, ready.at[answers[slot]], peers[slot]))

    def y_copy(d):
        return remote(
            fac_hbm.at[rows(color)], gathered.at[virt, rows(color)], y_send.at[d - 1], y_recv.at[d - 1], peers[slot_of(1, d)]
        )

    def z_copy(d):
        return remote(g_near.at[z], g_near.at[z], g_sem.at[0, d - 1], g_sem.at[1, d - 1], peers[slot_of(2, d)])

    def send_earlier(slot, copy):
        start_if(jnp.logical_not(later[slot]), copy)

    def send_later(slot, copy):
        ensure(slot)
        start_if(later[slot], copy)

    for d in ORDER:
        send_earlier(slot_of(1, d), y_copy(d))

    def dress(k, carry):
        direct, crossed = carry
        left = jnp.concatenate([ov_by_k[2 * k], ov_by_k[2 * k + 1]], axis=1)
        pair_rows = amp[pl.ds(pl.multiple_of(k * 2 * V, 2 * V), 2 * V), :]
        side = jnp.concatenate([pair_rows[:V], pair_rows[V:]], axis=1)
        return direct + dot_nt(left, side), crossed + dot_nn(left, pair_rows)

    zero = jnp.zeros((Q, V), F32)
    sums = (zero, zero)
    for n in range(PARTS):
        amp_load(n).wait()
        share = NOCC // 2 // PARTS
        sums = lax.fori_loop(n * share, (n + 1) * share, dress, sums, unroll=4)
    direct, crossed = sums
    dressed = (2.0 * direct - crossed).astype(BF16)
    lane = lax.broadcasted_iota(jnp.int32, (16, V), 1)
    line = lax.broadcasted_iota(jnp.int32, (16, V), 0)
    chip_rows = jnp.where(lane == y * 16 + line, 1.0, 0.0).astype(BF16)
    rows_out = dot_nt(chip_rows, dressed)
    rows_out = jnp.concatenate([rows_out, jnp.zeros((16, V - Q), F32)], axis=1).astype(BF16)
    g_near[z] = rows_out
    for d in ORDER:
        send_earlier(slot_of(2, d), z_copy(d))

    loads[0].wait()
    loads[1].wait()
    own_rows = jnp.where(lane == virt * W + line % W, 1.0, 0.0)
    fock_rows = dot_nt(own_rows.astype(BF16), fock[...])
    lhs[pl.ds(Q * W, 16), :] = jnp.where(line < W, fock_rows, own_rows).astype(BF16)

    def inter_step(jp, carry):
        both = dot_nt(lhs[...], amp[pl.ds(pl.multiple_of(jp * 2 * V, 2 * V), 2 * V), :])
        both = both.reshape(Q + 2, W, 2 * V)
        packed = jnp.concatenate([both[:, :, :V], both[:, :, V:]], axis=1).astype(BF16)
        inter[:, pl.ds(pl.multiple_of(jp * 16, 16), 16), :] = packed
        return carry

    part = NOCC // 8
    for n, group in enumerate(((1, 7), (2, 6), (3, 5), (4,))):
        lax.fori_loop(n * part, (n + 1) * part, inter_step, 0, unroll=8)
        for d in group:
            send_later(slot_of(1, d), y_copy(d))
    ensure(21)
    start(remote(fac_hbm, gathered.at[virt], own_sem.at[0], own_sem.at[1], sibling))
    even = z % 2 == 0
    ensure(slot_of(0, 1))
    ensure(slot_of(0, 7))
    pl.when(even)(functools.partial(ensure, slot_of(2, 1)))
    pl.when(jnp.logical_not(even))(functools.partial(ensure, slot_of(2, 7)))
    for d in ORDER:
        relay(d)

    pl.when(jnp.logical_not(even))(functools.partial(ensure, slot_of(2, 1)))
    pl.when(even)(functools.partial(ensure, slot_of(2, 7)))
    for d in range(1, NZ):
        if d not in (1, 7):
            ensure(slot_of(2, d))
        start_if(later[slot_of(2, d)], z_copy(d))

    for d in range(1, NZ):
        there = g_near.at[(z - d) % NZ]
        remote(there, there, g_sem.at[0, d - 1], g_sem.at[1, d - 1], sibling).wait_recv()

    def near_rows(n):
        wide = g_near[n].astype(F32)
        return jnp.where(core == 0, wide[:W], wide[W:])

    for m in range(NZ // 2):
        low, high = near_rows(m), near_rows(m + NZ // 2)
        both = jnp.concatenate([low[:, :Q], high[:, :Q]], axis=1)
        g_pack[pl.ds(m * W, W), :] = both
    g_far[x] = g_pack[...].astype(BF16)
    for d in range(2, NX - 1):
        ensure(slot_of(0, d))
    for d in range(1, NX):
        start(remote(g_far.at[x], g_far.at[x], g_sem.at[2, d - 1], g_sem.at[3, d - 1], peers[slot_of(0, d)]))
    for d in ORDER:
        relay_in_plane(d)

    picked = []
    own_mat = own_rows.astype(BF16)
    for n in range(NOCC // 4):
        four = dot_nt(own_mat, ov_by_k[4 * n : 4 * n + 4].reshape(4 * Q, V))[:W]
        picked += [four[:, :V], four[:, V:]]
    picked = jnp.concatenate(picked, axis=0).astype(BF16)

    def twice(block):
        empty = jnp.zeros((Q, V), BF16)
        top = jnp.concatenate([block, empty], axis=1)
        return jnp.concatenate([top, jnp.concatenate([empty, block], axis=1)], axis=0)

    cycle = dot_nn(picked, twice(dressed)).reshape(NOCC // 2, W, 2 * V)
    cycle = jnp.concatenate([cycle[:, :, :V], cycle[:, :, V:]], axis=1).reshape(NOCC * W, V)
    ov_mine = ov_wide[pl.ds(pair, Q, stride=NOCC), :].astype(BF16)

    def ladder(quarter):
        span = rows(quarter)
        first = pl.multiple_of(quarter % 4 * (Q // 4), Q // 4)
        for chip in range(NY):
            one = gathered[2 * chip, span, :].astype(F32).reshape(Q // 4, W, V)
            two = gathered[2 * chip + 1, span, :].astype(F32).reshape(Q // 4, W, V)
            weights[pl.ds(first, Q // 4), chip * 16 : chip * 16 + 16, :] = jnp.concatenate([one, two], axis=1).astype(BF16)
        for m in range(0, NOCC * W, 256):
            block = None
            for p in range(0, Q // 4, 2):
                left = [inter[first + p + n, m : m + 256] for n in range(2)]
                right = [weights[first + p + n] for n in range(2)]
                term = dot_nt(jnp.concatenate(left, axis=1), jnp.concatenate(right, axis=1))
                block = term if block is None else block + term
            total[m : m + 256] += block

    for m in range(0, NOCC * W, 256):
        block = dot_nt(inter[Q + 1, m : m + 256], fock[...])
        total[m : m + 256] = block + inter[Q, m : m + 256].astype(F32) + cycle[m : m + 256]
    loads[2].wait()
    other = gathered.at[y * 2 + 1 - core]
    remote(other, other, own_sem.at[0], own_sem.at[1], sibling).wait_recv()
    for d in ORDER:
        there = gathered.at[(y - d) % NY * 2 + 1 - core, rows(color)]
        remote(there, there, in_send.at[d - 1, 3], in_recv.at[d - 1, 3], sibling).wait_recv()
    ladder(color)

    for n in (1, 0, 2):
        for d in ORDER:
            there = gathered.at[(y - d) % NY * 2 + 1 - core, rows(color + 1 + n)]
            remote(there, there, sib_send.at[d - 1, n], sib_recv.at[d - 1, n], sibling).wait_recv()
        ladder(color + 1 + n)

    for d in range(1, NX):
        there = g_far.at[(x - d) % NX]
        remote(there, there, g_sem.at[2, d - 1], g_sem.at[3, d - 1], sibling).wait_recv()
    mirror = dot_nn(g_far[...].reshape(NX * NZ // 2 * W, V), twice(ov_mine))
    mirror = mirror.reshape(NX, NZ // 2, W, 2 * V)

    loads[3].wait()
    for j in range(0, NOCC, 2):
        tiles = []
        for k in (j, j + 1):
            jx, jz = k // NZ, k % NZ
            lanes = slice(jz // (NZ // 2) * V, (jz // (NZ // 2) + 1) * V)
            tile = total[k * W : (k + 1) * W] + mirror[jx, jz % (NZ // 2), :, lanes]
            tiles.append(tile * screen[0, k].astype(F32))
        out_ref[pl.ds(j * W, 16), :] = jnp.concatenate(tiles, axis=0).astype(BF16)

    for condition, copy in sends:
        if condition is None:
            copy.wait_send()
        else:
            pl.when(condition)(copy.wait_send)


def body(amplitudes, factors, ov_factors, fock_matrix, screen):
    vmem, dma = pltpu.VMEM, pltpu.SemaphoreType.DMA
    out = pl.pallas_call(
        kernel,
        out_shape=jax.ShapeDtypeStruct((NOCC * W, V), BF16),
        in_specs=[pl.BlockSpec(memory_space=pl.ANY)] * 5,
        out_specs=pl.BlockSpec(memory_space=pltpu.VMEM),
        scratch_shapes=[
            vmem((NOCC * V, V), BF16),
            vmem((Q * NOCC, V), BF16),
            vmem((Q * NOCC, V), F32),
            vmem((NOCC, Q, V), BF16),
            vmem((V, V), BF16),
            pltpu.SMEM((1, NOCC), jnp.int32),
            vmem(((Q + 2) * W, V), BF16),
            vmem((NY * 2, Q * W, V), BF16),
            vmem((Q + 2, NOCC * W, V), BF16),
            vmem((Q, V, V), BF16),
            vmem((NOCC * W, V), F32),
            vmem((NX, 16, V), BF16),
            vmem((NX // 2 * W, V), F32),
            vmem((NX, NZ // 2 * W, V), BF16),
            dma((6,)),
            dma((PARTS,)),
            dma((NY - 1,)),
            dma((NY - 1,)),
            dma((NY - 1, 4)),
            dma((NY - 1, 4)),
            dma((NY - 1, 3)),
            dma((NY - 1, 3)),
            dma((2,)),
            dma((4, NX - 1)),
            pltpu.SemaphoreType.REGULAR((22,)),
        ],
        compiler_params=pltpu.CompilerParams(
            collective_id=0, has_side_effects=True, vmem_limit_bytes=62 * 1024 * 1024
        ),
        name="residual",
    )(
        amplitudes.reshape(NOCC * V, V),
        factors.reshape(Q * W, V),
        ov_factors.reshape(Q * NOCC, V),
        fock_matrix,
        screen,
    )
    return out.reshape(NOCC, W, V)


def solution(mesh):
    in_specs = (P("pair", None, None), P(None, "virt", None), P(), P(), P("pair", None))
    out_specs = P("pair", "virt", None)
    return jax.shard_map(body, mesh=mesh, in_specs=in_specs, out_specs=out_specs, check_vma=False)
```

```python
import functools

import jax
import jax.numpy as jnp
from jax import lax
from jax.experimental import pallas as pl
from jax.experimental.pallas import tpu as pltpu
from jax.sharding import PartitionSpec as P

F32, BF16 = jnp.float32, jnp.bfloat16
MESH = pl.DeviceIdType.MESH
NX, NY, NZ = 8, 8, 8
V, Q, NOCC, W = 128, 64, 64, 8
QROWS = Q // 4 * W
PARTS = 4
ORDER = (1, 7, 2, 6, 3, 5, 4)
GROUPS = ((0, 4), (4, 7))


def dot_nt(a, b):
    return lax.dot_general(a, b, (((1,), (1,)), ((), ())), preferred_element_type=F32)


def dot_nn(a, b):
    return jnp.dot(a, b, preferred_element_type=F32)


def kernel(
    amp_hbm, fac_hbm, ov_hbm, fock_hbm, screen_hbm, out_ref,
    amp, ov_raw, ov_wide, ov_by_k, fock, screen, lhs, gathered, inter, weights,
    total, g_parts, g_near, g_pack, g_far,
    local_sem, ov_sem, amp_sem, part_sem, y_send, y_recv, in_send, in_recv, sib_send, sib_recv, own_sem, g_sem, ready,
):
    pair, virt = lax.axis_index("pair"), lax.axis_index("virt")
    x, z = pair // NZ, pair % NZ
    y, core = virt // 2, virt % 2
    color = (x + 2 * z) % 4
    sibling = (pair, y * 2 + 1 - core)

    def remote(src, dst, send, recv, device):
        return pltpu.make_async_remote_copy(
            src_ref=src, dst_ref=dst, send_sem=send, recv_sem=recv, device_id=device, device_id_type=MESH
        )

    def amp_load(n):
        number = (core * (PARTS // 2) + n) % PARTS
        span = pl.ds(pl.multiple_of(number * (NOCC * V // PARTS), NOCC * V // PARTS), NOCC * V // PARTS)
        return pltpu.make_async_copy(amp_hbm.at[span], amp.at[span], amp_sem.at[n])

    def ov_load(half):
        span = pl.ds(pl.multiple_of(half * (NOCC // 2), NOCC // 2), NOCC // 2)
        return pltpu.make_async_copy(ov_hbm.at[:, span], ov_raw.at[:, span], ov_sem.at[half])

    ov_load(core).start()
    for n in range(PARTS // 2):
        amp_load(n).start()
    ov_load(1 - core).start()
    for n in range(PARTS // 2, PARTS):
        amp_load(n).start()
    loads = [
        pltpu.make_async_copy(fock_hbm, fock, local_sem.at[2]),
        pltpu.make_async_copy(fac_hbm, gathered.at[:, core, NY - 1], local_sem.at[3]),
        pltpu.make_async_copy(screen_hbm, screen, local_sem.at[5]),
    ]
    for load in loads:
        load.start()

    def key(px, py, pz, pc):
        hops = jnp.minimum(px, NX - px) + jnp.minimum(py, NY - py)
        number = ((px * NZ + pz) * NY + py) * 2 + pc
        return jnp.where(number == 0, 9 * NZ // 2 * 1024 - 1, (pz * 9 + hops) * 1024 + number)

    mine = key(x, y, z, core)
    peers, answers, later = [], [], []
    for axis in range(3):
        for d in range(1, 8):
            at = [x, y, z]
            at[axis] = (at[axis] + d) % 8
            peers.append((at[0] * NZ + at[2], at[1] * 2 + core))
            answers.append(axis * 7 + 7 - d)
            later.append(key(*at, core) > mine)
    peers.append(sibling)
    answers.append(21)
    later.append(key(x, y, z, 1 - core) > mine)

    def signal(semaphore, device):
        pl.semaphore_signal(semaphore, inc=1, device_id=device, device_id_type=MESH)

    barrier = pltpu.get_barrier_semaphore()
    for peer, is_later in zip(peers, later):
        pl.when(is_later)(functools.partial(signal, barrier, peer))
    earlier_count = sum(jnp.where(is_later, 0, 1) for is_later in later)

    def ensure(slot):
        pl.when(later[slot])(functools.partial(pl.semaphore_wait, ready.at[slot], 1))

    def slot_of(axis, d):
        return axis * 7 + d - 1

    sends = []

    def start(copy):
        copy.start()
        sends.append((None, copy))

    def start_if(condition, copy):
        pl.when(condition)(copy.start)
        sends.append((condition, copy))

    def drain():
        for condition, copy in sends:
            if condition is None:
                copy.wait_send()
            else:
                pl.when(condition)(copy.wait_send)
        sends.clear()

    def block(quarter, which_core, group):
        return gathered.at[quarter % 4, which_core, pl.ds(group[0], group[1] - group[0])]

    def relay(g):
        group = GROUPS[g]
        for place in range(*group):
            there = gathered.at[color, core, place]
            remote(there, there, y_send.at[place], y_recv.at[place], sibling).wait_recv()
        piece = block(color, core, group)
        targets = ((x + 1) % NX * NZ + z, (x + NX - 1) % NX * NZ + z, x * NZ + z + 1 - z % 2 * 2)
        for way, target in enumerate(targets):
            start(remote(piece, piece, in_send.at[g, way], in_recv.at[g, way], (target, virt)))
        start(remote(piece, piece, in_send.at[g, 3], in_recv.at[g, 3], sibling))

    def relay_in_plane(copies):
        for n, way in ((1, 2), (0, 1), (2, 0)):
            for g in range(2):
                piece = block(color + 1 + n, core, GROUPS[g])
                remote(piece, piece, in_send.at[g, way], in_recv.at[g, way], sibling).wait_recv()
                copies.append(remote(piece, piece, sib_send.at[g, n], sib_recv.at[g, n], sibling))
                copies[-1].start()

    def y_copy(d):
        place = ORDER.index(d)
        there = gathered.at[color, core, place]
        return remote(fac_hbm.at[color], there, y_send.at[place], y_recv.at[place], peers[slot_of(1, d)])

    def z_copy(d):
        return remote(g_near.at[z], g_near.at[z], g_sem.at[0, d - 1], g_sem.at[1, d - 1], peers[slot_of(2, d)])

    def send_earlier(slot, copy):
        start_if(jnp.logical_not(later[slot]), copy)

    def send_later(slot, copy):
        ensure(slot)
        start_if(later[slot], copy)

    def answer(slot):
        signal(ready.at[answers[slot]], peers[slot])

    def enter():
        pl.when(earlier_count > 0)(functools.partial(pl.semaphore_wait, barrier, earlier_count))
        for slot in range(21, -1, -1):
            pl.when(jnp.logical_not(later[slot]))(functools.partial(answer, slot))
        for d in ORDER:
            pl.when(jnp.logical_not(later[slot_of(1, d)]))(y_copy(d).start)

    leading = (pair == 0) & (y == 0)
    pl.when(leading)(enter)

    def split(half):
        ov_load(half).wait()
        first = half * (NOCC // 2)
        raw = ov_raw[:, pl.ds(pl.multiple_of(first, NOCC // 2), NOCC // 2), :]
        span = pl.ds(pl.multiple_of(first * Q, NOCC // 2 * Q), NOCC // 2 * Q)
        ov_wide[span, :] = raw.astype(F32).reshape(NOCC // 2 * Q, V)

        def split_k(k, carry):
            ov_by_k[first + k] = ov_wide[pl.ds(first * Q + k, Q, stride=NOCC // 2), :].astype(BF16)
            return carry

        lax.fori_loop(0, NOCC // 2, split_k, 0, unroll=8)

    split(core)

    def dress(first, n, carry):
        k = first + n
        direct, crossed = carry
        left = jnp.concatenate([ov_by_k[2 * k], ov_by_k[2 * k + 1]], axis=1)
        pair_rows = amp[pl.ds(pl.multiple_of(k * 2 * V, 2 * V), 2 * V), :]
        side = jnp.concatenate([pair_rows[:V], pair_rows[V:]], axis=1)
        return direct + dot_nt(left, side), crossed + dot_nn(left, pair_rows)

    zero = jnp.zeros((Q, V), F32)
    sums = (zero, zero)
    share = NOCC // 2 // PARTS
    for n in range(PARTS // 2):
        amp_load(n).wait()
        first = core * (NOCC // 4) + n * share
        sums = lax.fori_loop(0, share, functools.partial(dress, first), sums, unroll=4)
    g_parts[0] = 2.0 * sums[0] - sums[1]

    pl.when(jnp.logical_not(leading))(enter)
    sends.extend((jnp.logical_not(later[slot_of(1, d)]), y_copy(d)) for d in ORDER)
    ensure(21)
    part_copy = remote(g_parts.at[0], g_parts.at[1], part_sem.at[0], part_sem.at[1], sibling)
    start(part_copy)
    start(remote(fac_hbm, gathered.at[:, core, NY - 1], own_sem.at[0], own_sem.at[1], sibling))
    part_copy.wait_recv()
    dressed = (g_parts[0] + g_parts[1]).astype(BF16)
    lane = lax.broadcasted_iota(jnp.int32, (16, V), 1)
    line = lax.broadcasted_iota(jnp.int32, (16, V), 0)
    chip_rows = jnp.where(lane == y * 16 + line, 1.0, 0.0).astype(BF16)
    rows_out = dot_nt(chip_rows, dressed)
    rows_out = jnp.concatenate([rows_out, jnp.zeros((16, V - Q), F32)], axis=1).astype(BF16)
    g_near[z] = rows_out
    for d in ORDER:
        send_earlier(slot_of(2, d), z_copy(d))

    loads[0].wait()
    loads[1].wait()
    lhs[pl.ds(0, Q * W), :] = gathered[:, core, NY - 1].reshape(Q * W, V)
    own_rows = jnp.where(lane == virt * W + line % W, 1.0, 0.0)
    fock_rows = dot_nt(own_rows.astype(BF16), fock[...])
    lhs[pl.ds(Q * W, 16), :] = jnp.where(line < W, fock_rows, own_rows).astype(BF16)

    def inter_step(jp, carry):
        both = dot_nt(lhs[...], amp[pl.ds(pl.multiple_of(jp * 2 * V, 2 * V), 2 * V), :])
        both = both.reshape(Q + 2, W, 2 * V)
        packed = jnp.concatenate([both[:, :, :V], both[:, :, V:]], axis=1).astype(BF16)
        inter[:, pl.ds(pl.multiple_of(jp * 16, 16), 16), :] = packed
        return carry

    for n in range(PARTS // 2, PARTS):
        amp_load(n).wait()
    part = NOCC // 8
    for n, group in enumerate(((1, 7), (2, 6), (3, 5), (4,))):
        lax.fori_loop(n * part, (n + 1) * part, inter_step, 0, unroll=8)
        for d in group:
            send_later(slot_of(1, d), y_copy(d))
    even = z % 2 == 0
    ensure(slot_of(0, 1))
    ensure(slot_of(0, 7))
    pl.when(even)(functools.partial(ensure, slot_of(2, 1)))
    pl.when(jnp.logical_not(even))(functools.partial(ensure, slot_of(2, 7)))
    for g in range(2):
        relay(g)

    split(1 - core)

    picked = []
    own_mat = own_rows.astype(BF16)
    for n in range(NOCC // 4):
        four = dot_nt(own_mat, ov_by_k[4 * n : 4 * n + 4].reshape(4 * Q, V))[:W]
        picked += [four[:, :V], four[:, V:]]
    picked = jnp.concatenate(picked, axis=0).astype(BF16)

    def twice(block):
        empty = jnp.zeros((Q, V), BF16)
        top = jnp.concatenate([block, empty], axis=1)
        return jnp.concatenate([top, jnp.concatenate([empty, block], axis=1)], axis=0)

    cycle = dot_nn(picked, twice(dressed)).reshape(NOCC // 2, W, 2 * V)
    cycle = jnp.concatenate([cycle[:, :, :V], cycle[:, :, V:]], axis=1).reshape(NOCC * W, V)
    half, number = pair // (NOCC // 2), pair % (NOCC // 2)
    ov_mine = ov_wide[pl.ds(half * (NOCC // 2 * Q) + number, Q, stride=NOCC // 2), :].astype(BF16)

    def ladder(quarter):
        first = pl.multiple_of(quarter % 4 * (Q // 4), Q // 4)
        for place in range(NY):
            chip = (y - (ORDER + (0,))[place]) % NY
            one, two = (gathered[quarter % 4, n, place].astype(F32).reshape(Q // 4, W, V) for n in range(2))
            both = jnp.concatenate([one, two], axis=1).astype(BF16)
            weights[pl.ds(first, Q // 4), pl.ds(pl.multiple_of(chip * 16, 16), 16), :] = both
        for m in range(0, NOCC * W, 256):
            part_sum = None
            for p in range(0, Q // 4, 2):
                left = [inter[first + p + n, m : m + 256] for n in range(2)]
                right = [weights[first + p + n] for n in range(2)]
                term = dot_nt(jnp.concatenate(left, axis=1), jnp.concatenate(right, axis=1))
                part_sum = term if part_sum is None else part_sum + term
            total[m : m + 256] += part_sum

    for m in range(0, NOCC * W, 256):
        fock_part = dot_nt(inter[Q + 1, m : m + 256], fock[...])
        total[m : m + 256] = fock_part + inter[Q, m : m + 256].astype(F32) + cycle[m : m + 256]
    other = gathered.at[:, 1 - core, NY - 1]
    remote(other, other, own_sem.at[0], own_sem.at[1], sibling).wait_recv()
    def plane_work():
        copies = []
        relay_in_plane(copies)
        for g in range(2):
            there = block(color, 1 - core, GROUPS[g])
            remote(there, there, in_send.at[g, 3], in_recv.at[g, 3], sibling).wait_recv()
        ladder(color)
        for n in (1, 0, 2):
            for g in range(2):
                there = block(color + 1 + n, 1 - core, GROUPS[g])
                remote(there, there, sib_send.at[g, n], sib_recv.at[g, n], sibling).wait_recv()
            ladder(color + 1 + n)
        for copy in copies:
            copy.wait_send()

    def to_leader(d):
        return later[slot_of(2, d)] & (z + d == NZ)

    def serve(d, ensured):
        if not ensured:
            pl.semaphore_wait(ready.at[slot_of(2, d)], 1)
        z_copy(d).start()

    for d in (5, 6, 7):
        pl.when(to_leader(d))(functools.partial(serve, d, d == 7))
    pl.when(jnp.logical_not(even))(functools.partial(ensure, slot_of(2, 1)))
    pl.when(even)(functools.partial(ensure, slot_of(2, 7)))
    for d in range(1, NZ):
        others = later[slot_of(2, d)] & (z + d != NZ)
        pl.when(others)(functools.partial(serve, d, d in (1, 7)))
        sends.append((later[slot_of(2, d)], z_copy(d)))

    for d in range(1, NZ):
        there = g_near.at[(z - d) % NZ]
        remote(there, there, g_sem.at[0, d - 1], g_sem.at[1, d - 1], sibling).wait_recv()

    def near_rows(n):
        wide = g_near[n].astype(F32)
        return jnp.where(core == 0, wide[:W], wide[W:])

    for m in range(NZ // 2):
        low, high = near_rows(m), near_rows(m + NZ // 2)
        both = jnp.concatenate([low[:, :Q], high[:, :Q]], axis=1)
        g_pack[pl.ds(m * W, W), :] = both
    g_far[x] = g_pack[...].astype(BF16)
    for d in range(2, NX - 1):
        ensure(slot_of(0, d))
    for d in range(1, NX):
        start(remote(g_far.at[x], g_far.at[x], g_sem.at[2, d - 1], g_sem.at[3, d - 1], peers[slot_of(0, d)]))

    plane_work()

    drain()
    for d in range(1, NX):
        there = g_far.at[(x - d) % NX]
        remote(there, there, g_sem.at[2, d - 1], g_sem.at[3, d - 1], sibling).wait_recv()
    mirror = dot_nn(g_far[...].reshape(NX * NZ // 2 * W, V), twice(ov_mine))
    mirror = mirror.reshape(NX, NZ // 2, W, 2 * V)

    loads[2].wait()
    for j in range(0, NOCC, 2):
        tiles = []
        for k in (j, j + 1):
            jx, jz = k // NZ, k % NZ
            lanes = slice(jz // (NZ // 2) * V, (jz // (NZ // 2) + 1) * V)
            tile = total[k * W : (k + 1) * W] + mirror[jx, jz % (NZ // 2), :, lanes]
            tiles.append(tile * screen[0, k].astype(F32))
        out_ref[pl.ds(j * W, 16), :] = jnp.concatenate(tiles, axis=0).astype(BF16)

    drain()


def body(amplitudes, factors, ov_factors, fock_matrix, screen):
    vmem, dma = pltpu.VMEM, pltpu.SemaphoreType.DMA
    out = pl.pallas_call(
        kernel,
        out_shape=jax.ShapeDtypeStruct((NOCC * W, V), BF16),
        in_specs=[pl.BlockSpec(memory_space=pl.ANY)] * 5,
        out_specs=pl.BlockSpec(memory_space=pltpu.VMEM),
        scratch_shapes=[
            vmem((NOCC * V, V), BF16),
            vmem((Q, NOCC, V), BF16),
            vmem((Q * NOCC, V), F32),
            vmem((NOCC, Q, V), BF16),
            vmem((V, V), BF16),
            pltpu.SMEM((1, NOCC), jnp.int32),
            vmem(((Q + 2) * W, V), BF16),
            vmem((4, 2, NY, QROWS, V), BF16),
            vmem((Q + 2, NOCC * W, V), BF16),
            vmem((Q, V, V), BF16),
            vmem((NOCC * W, V), F32),
            vmem((2, Q, V), F32),
            vmem((NX, 16, V), BF16),
            vmem((NX // 2 * W, V), F32),
            vmem((NX, NZ // 2 * W, V), BF16),
            dma((6,)),
            dma((2,)),
            dma((PARTS,)),
            dma((2,)),
            dma((NY - 1,)),
            dma((NY - 1,)),
            dma((2, 4)),
            dma((2, 4)),
            dma((2, 3)),
            dma((2, 3)),
            dma((2,)),
            dma((4, NX - 1)),
            pltpu.SemaphoreType.REGULAR((22,)),
        ],
        compiler_params=pltpu.CompilerParams(
            collective_id=0, has_side_effects=True, vmem_limit_bytes=62 * 1024 * 1024
        ),
        name="residual",
    )(
        amplitudes.reshape(NOCC * V, V),
        factors.reshape(4, QROWS, V),
        ov_factors,
        fock_matrix,
        screen,
    )
    return out.reshape(NOCC, W, V)


def solution(mesh):
    in_specs = (P("pair", None, None), P(None, "virt", None), P(), P(), P("pair", None))
    out_specs = P("pair", "virt", None)
    return jax.shard_map(body, mesh=mesh, in_specs=in_specs, out_specs=out_specs, check_vma=False)
```

```python
import functools

import jax
import jax.numpy as jnp
from jax import lax
from jax.experimental import pallas as pl
from jax.experimental.pallas import tpu as pltpu
from jax.sharding import PartitionSpec as P

F32, BF16 = jnp.float32, jnp.bfloat16
MESH = pl.DeviceIdType.MESH
NX, NY, NZ = 8, 8, 8
V, Q, NOCC, W = 128, 64, 64, 8
QROWS = Q // 4 * W
PARTS = 4
ORDER = (1, 7, 2, 6, 3, 5, 4)
GROUPS = ((0, 4), (4, 7))


def dot_nt(a, b):
    return lax.dot_general(a, b, (((1,), (1,)), ((), ())), preferred_element_type=F32)


def dot_nn(a, b):
    return jnp.dot(a, b, preferred_element_type=F32)


def kernel(
    amp_hbm, fac_hbm, ov_hbm, fock_hbm, screen_hbm, out_ref,
    amp, ov_raw, ov_wide, ov_by_k, fock, screen, lhs, gathered, inter, weights,
    total, g_parts, g_near, g_pack, g_far,
    local_sem, ov_sem, amp_sem, part_sem, y_send, y_recv, in_send, in_recv, sib_send, sib_recv, own_sem, g_sem, ready,
):
    pair, virt = lax.axis_index("pair"), lax.axis_index("virt")
    x, z = pair // NZ, pair % NZ
    y, core = virt // 2, virt % 2
    color = (x + 2 * z) % 4
    sibling = (pair, y * 2 + 1 - core)

    def remote(src, dst, send, recv, device):
        return pltpu.make_async_remote_copy(
            src_ref=src, dst_ref=dst, send_sem=send, recv_sem=recv, device_id=device, device_id_type=MESH
        )

    def amp_load(n):
        number = (core * (PARTS // 2) + n) % PARTS
        span = pl.ds(pl.multiple_of(number * (NOCC * V // PARTS), NOCC * V // PARTS), NOCC * V // PARTS)
        return pltpu.make_async_copy(amp_hbm.at[span], amp.at[span], amp_sem.at[n])

    def ov_load(half):
        span = pl.ds(pl.multiple_of(half * (NOCC // 2), NOCC // 2), NOCC // 2)
        return pltpu.make_async_copy(ov_hbm.at[:, span], ov_raw.at[:, span], ov_sem.at[half])

    ov_load(core).start()
    for n in range(PARTS // 2):
        amp_load(n).start()
    ov_load(1 - core).start()
    for n in range(PARTS // 2, PARTS):
        amp_load(n).start()
    loads = [
        pltpu.make_async_copy(fock_hbm, fock, local_sem.at[2]),
        pltpu.make_async_copy(fac_hbm, gathered.at[:, core, NY - 1], local_sem.at[3]),
        pltpu.make_async_copy(screen_hbm, screen, local_sem.at[5]),
    ]
    for load in loads:
        load.start()

    def key(px, py, pz, pc):
        hops = jnp.minimum(px, NX - px) + jnp.minimum(py, NY - py)
        number = ((px * NZ + pz) * NY + py) * 2 + pc
        return jnp.where(number == 0, 9 * NZ // 2 * 1024 - 1, (pz * 9 + hops) * 1024 + number)

    mine = key(x, y, z, core)
    peers, answers, later = [], [], []
    for axis in range(3):
        for d in range(1, 8):
            at = [x, y, z]
            at[axis] = (at[axis] + d) % 8
            peers.append((at[0] * NZ + at[2], at[1] * 2 + core))
            answers.append(axis * 7 + 7 - d)
            later.append(key(*at, core) > mine)
    peers.append(sibling)
    answers.append(21)
    later.append(key(x, y, z, 1 - core) > mine)

    def signal(semaphore, device):
        pl.semaphore_signal(semaphore, inc=1, device_id=device, device_id_type=MESH)

    barrier = pltpu.get_barrier_semaphore()
    for peer, is_later in zip(peers, later):
        pl.when(is_later)(functools.partial(signal, barrier, peer))
    earlier_count = sum(jnp.where(is_later, 0, 1) for is_later in later)

    def ensure(slot):
        pl.when(later[slot])(functools.partial(pl.semaphore_wait, ready.at[slot], 1))

    def slot_of(axis, d):
        return axis * 7 + d - 1

    sends = []

    def start(copy):
        copy.start()
        sends.append((None, copy))

    def start_if(condition, copy):
        pl.when(condition)(copy.start)
        sends.append((condition, copy))

    def drain():
        for condition, copy in sends:
            if condition is None:
                copy.wait_send()
            else:
                pl.when(condition)(copy.wait_send)
        sends.clear()

    def block(quarter, which_core, group):
        return gathered.at[quarter % 4, which_core, pl.ds(group[0], group[1] - group[0])]

    def relay(g):
        group = GROUPS[g]
        for place in range(*group):
            there = gathered.at[color, core, place]
            remote(there, there, y_send.at[place], y_recv.at[place], sibling).wait_recv()
        piece = block(color, core, group)
        targets = ((x + 1) % NX * NZ + z, (x + NX - 1) % NX * NZ + z, x * NZ + z + 1 - z % 2 * 2)
        for way, target in enumerate(targets):
            start(remote(piece, piece, in_send.at[g, way], in_recv.at[g, way], (target, virt)))
        start(remote(piece, piece, in_send.at[g, 3], in_recv.at[g, 3], sibling))

    def relay_in_plane(g, copies):
        for n, way in ((1, 2), (0, 1), (2, 0)):
            piece = block(color + 1 + n, core, GROUPS[g])
            remote(piece, piece, in_send.at[g, way], in_recv.at[g, way], sibling).wait_recv()
            copies[n].start()

    to_sibling = []
    for g in range(2):
        pieces = [block(color + 1 + n, core, GROUPS[g]) for n in range(3)]
        to_sibling.append([remote(p, p, sib_send.at[g, n], sib_recv.at[g, n], sibling) for n, p in enumerate(pieces)])

    def y_copy(d):
        place = ORDER.index(d)
        there = gathered.at[color, core, place]
        return remote(fac_hbm.at[color], there, y_send.at[place], y_recv.at[place], peers[slot_of(1, d)])

    def z_copy(d):
        return remote(g_near.at[z], g_near.at[z], g_sem.at[0, d - 1], g_sem.at[1, d - 1], peers[slot_of(2, d)])

    def send_earlier(slot, copy):
        start_if(jnp.logical_not(later[slot]), copy)

    def send_later(slot, copy):
        ensure(slot)
        start_if(later[slot], copy)

    def answer(slot):
        signal(ready.at[answers[slot]], peers[slot])

    def enter():
        pl.when(earlier_count > 0)(functools.partial(pl.semaphore_wait, barrier, earlier_count))
        for slot in range(21, -1, -1):
            pl.when(jnp.logical_not(later[slot]))(functools.partial(answer, slot))
        for d in ORDER:
            pl.when(jnp.logical_not(later[slot_of(1, d)]))(y_copy(d).start)

    leading = (pair == 0) & (y == 0)
    pl.when(leading)(enter)

    def split(half):
        ov_load(half).wait()
        first = half * (NOCC // 2)
        raw = ov_raw[:, pl.ds(pl.multiple_of(first, NOCC // 2), NOCC // 2), :]
        span = pl.ds(pl.multiple_of(first * Q, NOCC // 2 * Q), NOCC // 2 * Q)
        ov_wide[span, :] = raw.astype(F32).reshape(NOCC // 2 * Q, V)

        def split_k(k, carry):
            ov_by_k[first + k] = ov_wide[pl.ds(first * Q + k, Q, stride=NOCC // 2), :].astype(BF16)
            return carry

        lax.fori_loop(0, NOCC // 2, split_k, 0, unroll=8)

    split(core)

    def dress(first, n, carry):
        k = first + n
        direct, crossed = carry
        left = jnp.concatenate([ov_by_k[2 * k], ov_by_k[2 * k + 1]], axis=1)
        pair_rows = amp[pl.ds(pl.multiple_of(k * 2 * V, 2 * V), 2 * V), :]
        side = jnp.concatenate([pair_rows[:V], pair_rows[V:]], axis=1)
        return direct + dot_nt(left, side), crossed + dot_nn(left, pair_rows)

    zero = jnp.zeros((Q, V), F32)
    sums = (zero, zero)
    share = NOCC // 2 // PARTS
    for n in range(PARTS // 2):
        amp_load(n).wait()
        first = core * (NOCC // 4) + n * share
        sums = lax.fori_loop(0, share, functools.partial(dress, first), sums, unroll=4)
    g_parts[0] = 2.0 * sums[0] - sums[1]

    pl.when(jnp.logical_not(leading))(enter)
    sends.extend((jnp.logical_not(later[slot_of(1, d)]), y_copy(d)) for d in ORDER)
    ensure(21)
    part_copy = remote(g_parts.at[0], g_parts.at[1], part_sem.at[0], part_sem.at[1], sibling)
    start(part_copy)
    start(remote(fac_hbm, gathered.at[:, core, NY - 1], own_sem.at[0], own_sem.at[1], sibling))
    part_copy.wait_recv()
    dressed = (g_parts[0] + g_parts[1]).astype(BF16)
    lane = lax.broadcasted_iota(jnp.int32, (16, V), 1)
    line = lax.broadcasted_iota(jnp.int32, (16, V), 0)
    chip_rows = jnp.where(lane == y * 16 + line, 1.0, 0.0).astype(BF16)
    rows_out = dot_nt(chip_rows, dressed)
    rows_out = jnp.concatenate([rows_out, jnp.zeros((16, V - Q), F32)], axis=1).astype(BF16)
    g_near[z] = rows_out
    for d in ORDER:
        send_earlier(slot_of(2, d), z_copy(d))

    loads[0].wait()
    loads[1].wait()
    lhs[pl.ds(0, Q * W), :] = gathered[:, core, NY - 1].reshape(Q * W, V)
    own_rows = jnp.where(lane == virt * W + line % W, 1.0, 0.0)
    fock_rows = dot_nt(own_rows.astype(BF16), fock[...])
    lhs[pl.ds(Q * W, 16), :] = jnp.where(line < W, fock_rows, own_rows).astype(BF16)

    def inter_step(jp, carry):
        both = dot_nt(lhs[...], amp[pl.ds(pl.multiple_of(jp * 2 * V, 2 * V), 2 * V), :])
        both = both.reshape(Q + 2, W, 2 * V)
        packed = jnp.concatenate([both[:, :, :V], both[:, :, V:]], axis=1).astype(BF16)
        inter[:, pl.ds(pl.multiple_of(jp * 16, 16), 16), :] = packed
        return carry

    for n in range(PARTS // 2, PARTS):
        amp_load(n).wait()
    part = NOCC // 8
    for n, group in enumerate(((1, 7), (2, 6), (3, 5), (4,))):
        lax.fori_loop(n * part, (n + 1) * part, inter_step, 0, unroll=8)
        for d in group:
            send_later(slot_of(1, d), y_copy(d))
    even = z % 2 == 0
    ensure(slot_of(0, 1))
    ensure(slot_of(0, 7))
    pl.when(even)(functools.partial(ensure, slot_of(2, 1)))
    pl.when(jnp.logical_not(even))(functools.partial(ensure, slot_of(2, 7)))
    for g in range(2):
        relay(g)

    split(1 - core)

    picked = []
    own_mat = own_rows.astype(BF16)
    for n in range(NOCC // 4):
        four = dot_nt(own_mat, ov_by_k[4 * n : 4 * n + 4].reshape(4 * Q, V))[:W]
        picked += [four[:, :V], four[:, V:]]
    picked = jnp.concatenate(picked, axis=0).astype(BF16)

    def twice(block):
        empty = jnp.zeros((Q, V), BF16)
        top = jnp.concatenate([block, empty], axis=1)
        return jnp.concatenate([top, jnp.concatenate([empty, block], axis=1)], axis=0)

    cycle = dot_nn(picked, twice(dressed)).reshape(NOCC // 2, W, 2 * V)
    cycle = jnp.concatenate([cycle[:, :, :V], cycle[:, :, V:]], axis=1).reshape(NOCC * W, V)
    half, number = pair // (NOCC // 2), pair % (NOCC // 2)
    ov_mine = ov_wide[pl.ds(half * (NOCC // 2 * Q) + number, Q, stride=NOCC // 2), :].astype(BF16)

    def ladder(quarter):
        first = pl.multiple_of(quarter % 4 * (Q // 4), Q // 4)
        for place in range(NY):
            chip = (y - (ORDER + (0,))[place]) % NY
            one, two = (gathered[quarter % 4, n, place].astype(F32).reshape(Q // 4, W, V) for n in range(2))
            both = jnp.concatenate([one, two], axis=1).astype(BF16)
            weights[pl.ds(first, Q // 4), pl.ds(pl.multiple_of(chip * 16, 16), 16), :] = both
        for m in range(0, NOCC * W, 256):
            part_sum = None
            for p in range(0, Q // 4, 2):
                left = [inter[first + p + n, m : m + 256] for n in range(2)]
                right = [weights[first + p + n] for n in range(2)]
                term = dot_nt(jnp.concatenate(left, axis=1), jnp.concatenate(right, axis=1))
                part_sum = term if part_sum is None else part_sum + term
            total[m : m + 256] += part_sum

    for m in range(0, NOCC * W, 256):
        fock_part = dot_nt(inter[Q + 1, m : m + 256], fock[...])
        total[m : m + 256] = fock_part + inter[Q, m : m + 256].astype(F32) + cycle[m : m + 256]
    other = gathered.at[:, 1 - core, NY - 1]
    remote(other, other, own_sem.at[0], own_sem.at[1], sibling).wait_recv()
    def plane_work():
        pl.when(z > 0)(functools.partial(relay_in_plane, 0, to_sibling[0]))
        relay_in_plane(1, to_sibling[1])
        for g in range(2):
            there = block(color, 1 - core, GROUPS[g])
            remote(there, there, in_send.at[g, 3], in_recv.at[g, 3], sibling).wait_recv()
        ladder(color)
        for n in (1, 0, 2):
            for g in range(2):
                there = block(color + 1 + n, 1 - core, GROUPS[g])
                remote(there, there, sib_send.at[g, n], sib_recv.at[g, n], sibling).wait_recv()
            ladder(color + 1 + n)
        for copy in to_sibling[0] + to_sibling[1]:
            copy.wait_send()

    pl.when(z == 0)(functools.partial(relay_in_plane, 0, to_sibling[0]))

    def to_leader(d):
        return later[slot_of(2, d)] & (z + d == NZ)

    def serve(d, ensured):
        if not ensured:
            pl.semaphore_wait(ready.at[slot_of(2, d)], 1)
        z_copy(d).start()

    for d in (5, 6, 7):
        pl.when(to_leader(d))(functools.partial(serve, d, d == 7))
    pl.when(jnp.logical_not(even))(functools.partial(ensure, slot_of(2, 1)))
    pl.when(even)(functools.partial(ensure, slot_of(2, 7)))
    for d in range(1, NZ):
        others = later[slot_of(2, d)] & (z + d != NZ)
        pl.when(others)(functools.partial(serve, d, d in (1, 7)))
        sends.append((later[slot_of(2, d)], z_copy(d)))

    for d in range(1, NZ):
        there = g_near.at[(z - d) % NZ]
        remote(there, there, g_sem.at[0, d - 1], g_sem.at[1, d - 1], sibling).wait_recv()

    def near_rows(n):
        wide = g_near[n].astype(F32)
        return jnp.where(core == 0, wide[:W], wide[W:])

    for m in range(NZ // 2):
        low, high = near_rows(m), near_rows(m + NZ // 2)
        both = jnp.concatenate([low[:, :Q], high[:, :Q]], axis=1)
        g_pack[pl.ds(m * W, W), :] = both
    g_far[x] = g_pack[...].astype(BF16)
    for d in range(2, NX - 1):
        ensure(slot_of(0, d))
    for d in range(1, NX):
        start(remote(g_far.at[x], g_far.at[x], g_sem.at[2, d - 1], g_sem.at[3, d - 1], peers[slot_of(0, d)]))

    plane_work()

    drain()
    for d in range(1, NX):
        there = g_far.at[(x - d) % NX]
        remote(there, there, g_sem.at[2, d - 1], g_sem.at[3, d - 1], sibling).wait_recv()
    mirror = dot_nn(g_far[...].reshape(NX * NZ // 2 * W, V), twice(ov_mine))
    mirror = mirror.reshape(NX, NZ // 2, W, 2 * V)

    loads[2].wait()
    for j in range(0, NOCC, 2):
        tiles = []
        for k in (j, j + 1):
            jx, jz = k // NZ, k % NZ
            lanes = slice(jz // (NZ // 2) * V, (jz // (NZ // 2) + 1) * V)
            tile = total[k * W : (k + 1) * W] + mirror[jx, jz % (NZ // 2), :, lanes]
            tiles.append(tile * screen[0, k].astype(F32))
        out_ref[pl.ds(j * W, 16), :] = jnp.concatenate(tiles, axis=0).astype(BF16)

    drain()


def body(amplitudes, factors, ov_factors, fock_matrix, screen):
    vmem, dma = pltpu.VMEM, pltpu.SemaphoreType.DMA
    out = pl.pallas_call(
        kernel,
        out_shape=jax.ShapeDtypeStruct((NOCC * W, V), BF16),
        in_specs=[pl.BlockSpec(memory_space=pl.ANY)] * 5,
        out_specs=pl.BlockSpec(memory_space=pltpu.VMEM),
        scratch_shapes=[
            vmem((NOCC * V, V), BF16),
            vmem((Q, NOCC, V), BF16),
            vmem((Q * NOCC, V), F32),
            vmem((NOCC, Q, V), BF16),
            vmem((V, V), BF16),
            pltpu.SMEM((1, NOCC), jnp.int32),
            vmem(((Q + 2) * W, V), BF16),
            vmem((4, 2, NY, QROWS, V), BF16),
            vmem((Q + 2, NOCC * W, V), BF16),
            vmem((Q, V, V), BF16),
            vmem((NOCC * W, V), F32),
            vmem((2, Q, V), F32),
            vmem((NX, 16, V), BF16),
            vmem((NX // 2 * W, V), F32),
            vmem((NX, NZ // 2 * W, V), BF16),
            dma((6,)),
            dma((2,)),
            dma((PARTS,)),
            dma((2,)),
            dma((NY - 1,)),
            dma((NY - 1,)),
            dma((2, 4)),
            dma((2, 4)),
            dma((2, 3)),
            dma((2, 3)),
            dma((2,)),
            dma((4, NX - 1)),
            pltpu.SemaphoreType.REGULAR((22,)),
        ],
        compiler_params=pltpu.CompilerParams(
            collective_id=0, has_side_effects=True, vmem_limit_bytes=62 * 1024 * 1024
        ),
        name="residual",
    )(
        amplitudes.reshape(NOCC * V, V),
        factors.reshape(4, QROWS, V),
        ov_factors,
        fock_matrix,
        screen,
    )
    return out.reshape(NOCC, W, V)


def solution(mesh):
    in_specs = (P("pair", None, None), P(None, "virt", None), P(), P(), P("pair", None))
    out_specs = P("pair", "virt", None)
    return jax.shard_map(body, mesh=mesh, in_specs=in_specs, out_specs=out_specs, check_vma=False)
```
